32 devices in a mesh: row: 4 (over z), col: 8 (over y, x, core).
Axes of the slice: x: 2, y: 2, z: 4, core: 2. Of those that a mesh axis runs over, the one named last changes fastest.
Arguments:
- seq_ids: int32 [1024], replicated, may hold values from 0 to 7, never falling along the last dimension, each value on 1 to 192 neighbouring positions
- attn_weights: float32 [1024, 64, 32], P(('row', 'col')), may hold values from 0.05 to 20
- values: bfloat16 [1024, 8192], P(('row', 'col')), may hold values from -6 to 6
- out_grads: bfloat16 [1024, 8192], P(('row', 'col')), may hold values from -2 to 2
- act_basis: bfloat16 [8192, 8192], P('row', 'col'), may hold values from -0.0625 to 0.0625
- grad_basis: bfloat16 [8192, 8192], P('col', 'row'), may hold values from -0.0625 to 0.0625
Outputs:
- eigenvalues: float32 [8192, 8192], P('row', 'col')
The draws below stay inside these ranges and needn't reach their ends.
Inputs may be any that keep to these rules, and one draw needn't show every extreme that they name: `seq_ids`: ids never fall along the tokens; each of the 8 sequences is one run of 1 to 192 tokens, and one has exactly 192.
All inputs are finite; a program needn't handle non-finite values.
Results may differ from the reference program's by a relative error of at most 0.014.
Values may be sent and summed in bfloat16 or wider, within the bound.
A program may use at most 128 MiB of HBM per device.

```python
import math
import jax
import jax.numpy as jnp
import numpy as np
from jax import lax

HEADS = 64
HEAD = 128
D = 8192
WIN = 32
LONGEST = 192
TOKENS = 1024
SEQS = 8
N_ROW = 4
N_COL = 8


def levels(rng, shape, pieces, smallest, largest):
    factor_of, own = 1.0, jax.random.fold_in(rng, 6)
    for dim, parts in pieces:
        heights = jnp.exp(jax.random.uniform(jax.random.fold_in(own, dim), (parts,), jnp.float32, smallest / len(pieces), largest / len(pieces)))
        factor_of = factor_of * jnp.repeat(heights, shape[dim] // parts).reshape([-1 if axis == dim else 1 for axis in range(len(shape))])
    return factor_of


def split_up(amount, total, bound, slope):
    weights = [(1 << 20) // math.isqrt(grade ** slope) + 1 for grade in range(2, amount + 1)]
    rest, counts = total - bound - (amount - 1), [1] * (amount - 1)
    while rest > 0:
        movable = [i for i in range(amount - 1) if counts[i] < bound]
        mass, budget = sum([weights[i] for i in movable]), rest
        for i in movable:
            extra = min(bound - counts[i], max(1, budget * weights[i] // mass), rest)
            counts[i] = counts[i] + extra
            rest = rest - extra
    return np.array([bound] + counts)


def uneven_parts(rng, number_of, total, bound, lean):
    if number_of == 2:
        one = jax.random.randint(rng, (), max(1, total - bound), min(bound, total - 1) + 1)
        return jnp.stack([one, total - one])
    tallies = jnp.asarray(split_up(number_of, total, bound, lean), jnp.int32)
    pairs = (number_of - 1) // 2
    source_of, taker = tallies[1:1 + 2 * pairs:2], tallies[2:2 + 2 * pairs:2]
    margin = jnp.minimum(source_of - 1, bound - taker)
    passed = jax.random.randint(jax.random.fold_in(rng, 1), (pairs,), 0, 1 << 20) % (margin + 1)
    tallies = tallies.at[1:1 + 2 * pairs:2].set(source_of - passed).at[2:2 + 2 * pairs:2].set(taker + passed)
    return tallies[jax.random.permutation(jax.random.fold_in(rng, 2), number_of)]


def gaussian(key, shape, width, limit, pieces=(), held_as=jnp.bfloat16):
    gain = levels(key, shape, pieces, -0.22, 0.18) if pieces else 1.0
    result = jax.random.normal(key, shape, jnp.float32) * width * gain
    return jnp.minimum(jnp.maximum(result, -limit), limit).astype(held_as)


def setup_inputs(seed: int = 0) -> dict:
    key_list = jax.random.split(jax.random.key(seed), 7)
    seq_ids = jnp.searchsorted(jnp.cumsum(uneven_parts(key_list[0], SEQS, TOKENS, LONGEST, 1)), jnp.arange(TOKENS), side="right").astype(jnp.int32)
    attn_weights = jnp.clip(jnp.exp(math.log(20.0) - 5.9914645 * jax.random.uniform(key_list[1], (TOKENS, HEADS, WIN), jnp.float32) ** levels(key_list[1], (TOKENS, HEADS, WIN), ((0, 32),), -0.2, 0.2)), 0.05, 20.0)
    values = gaussian(key_list[2], (TOKENS, D), 1.0, 6.0, ((0, 32),))
    out_grads = gaussian(key_list[3], (TOKENS, D), 0.25, 2.0, ((0, 32),))
    act_basis = gaussian(key_list[4], (D, D), D ** -0.5, 0.0625, ((0, 4), (1, 8)))
    grad_basis = gaussian(key_list[5], (D, D), D ** -0.5, 0.0625, ((0, 8), (1, 4)))
    return {"seq_ids": seq_ids, "attn_weights": attn_weights, "values": values, "out_grads": out_grads, "act_basis": act_basis, "grad_basis": grad_basis}


def blocked_rotate(data, basis, blocks):
    size = D // blocks
    total = jnp.zeros((data.shape[0], basis.shape[1]), jnp.float32)
    for block in range(blocks):
        part = jnp.dot(data[:, block * size:(block + 1) * size].astype(jnp.float32), basis[block * size:(block + 1) * size, :].astype(jnp.float32))
        total = total + part.astype(jnp.bfloat16).astype(jnp.float32)
    return total.astype(jnp.bfloat16)


def reference(seq_ids, attn_weights, values, out_grads, act_basis, grad_basis):
    positions = jnp.arange(TOKENS, dtype=jnp.int32)
    offsets = jnp.arange(WIN, dtype=jnp.int32)
    key_pos = positions[:, None] - offsets[None, :]
    key_seg = seq_ids[jnp.clip(key_pos, 0, TOKENS - 1)]
    valid = jnp.logical_and(key_pos >= 0, key_seg == seq_ids[:, None]).astype(jnp.float32)
    masked = attn_weights * valid[:, None, :]
    probs = (masked / jnp.sum(masked, axis=2, keepdims=True)).astype(jnp.bfloat16)
    padded = jnp.concatenate([jnp.zeros((WIN, D), jnp.bfloat16), values], axis=0)
    mixed = jnp.zeros((TOKENS, HEADS, HEAD), jnp.float32)
    for step in range(WIN):
        shifted = padded[WIN - step:WIN - step + TOKENS].reshape(TOKENS, HEADS, HEAD).astype(jnp.float32)
        mixed = mixed + probs[:, :, step][:, :, None].astype(jnp.float32) * shifted
    inputs = mixed.reshape(TOKENS, D).astype(jnp.bfloat16)
    rot_inputs = blocked_rotate(inputs, act_basis, N_ROW)
    rot_grads = blocked_rotate(out_grads, grad_basis, N_COL)
    seq_range = jnp.arange(SEQS, dtype=jnp.int32)
    starts = jnp.sum((seq_ids[None, :] < seq_range[:, None]).astype(jnp.int32), axis=1).astype(jnp.int32)

    def accumulate(index, total):
        first = jnp.minimum(starts[index], TOKENS - LONGEST).astype(jnp.int32)
        grad_win = lax.dynamic_slice_in_dim(rot_grads, first, LONGEST, 0).astype(jnp.float32)
        act_win = lax.dynamic_slice_in_dim(rot_inputs, first, LONGEST, 0).astype(jnp.float32)
        seg_win = lax.dynamic_slice_in_dim(seq_ids, first, LONGEST, 0)
        grad_win = jnp.where((seg_win == index)[:, None], grad_win, jnp.float32(0.0))
        tile = jnp.dot(grad_win.T, act_win)
        return total + tile * tile

    total = lax.fori_loop(0, SEQS, accumulate, jnp.zeros((D, D), jnp.float32))
    return total / SEQS
```

```python
import functools
import jax
import jax.numpy as jnp
from jax import lax
from jax.experimental import pallas as pl
from jax.experimental.pallas import tpu as pltpu
from jax.sharding import PartitionSpec as P

SEQ_MEAN = 128
LONGEST = 192
MIB = 1 << 20


def from_behind(value, axis, steps):
    count = lax.axis_size(axis)
    initial, last = (max(0, -steps), min(count, count - steps))
    return lax.ppermute(value, axis, [(source, source + steps) for source in range(initial, last)])


def fit_kernel(sequences, window, bounds_ref, grads_ref, acts_ref, out_ref):
    total_tok = grads_ref.shape[0]
    positions = lax.broadcasted_iota(jnp.int32, (window, 1), 0)

    def tile(index):
        start, end = bounds_ref[index], bounds_ref[index + 1]
        first = pl.multiple_of(jnp.minimum(start // 16 * 16, total_tok - window), 16)
        here = positions + first
        inside = jnp.logical_and(here >= start, here < end)
        grads = grads_ref[pl.ds(first, window), :]
        grads = jnp.where(inside, grads, jnp.zeros_like(grads))
        acts = acts_ref[pl.ds(first, window), :]
        product = lax.dot_general(
            grads, acts, (((0,), (0,)), ((), ())), preferred_element_type=jnp.float32
        )
        return product * product

    out_ref[...] = tile(0)

    @pl.loop(1, sequences - 1)
    def _(index):
        out_ref[...] += tile(index)

    out_ref[...] = (out_ref[...] + tile(sequences - 1)) * (1.0 / sequences)


def fit(bounds, rot_grads, rot_inputs, sequences):
    total_tok, rows = rot_grads.shape
    columns = rot_inputs.shape[1]
    height = 256
    window = (LONGEST + 15 + 127) // 128 * 128
    return pl.pallas_call(
        functools.partial(fit_kernel, sequences, window),
        grid=(rows // height,),
        out_shape=jax.ShapeDtypeStruct((rows, columns), jnp.float32),
        in_specs=[
            pl.BlockSpec(memory_space=pltpu.SMEM),
            pl.BlockSpec((total_tok, height), lambda i: (0, i)),
            pl.BlockSpec((total_tok, columns), lambda i: (0, 0)),
        ],
        out_specs=pl.BlockSpec((height, columns), lambda i: (i, 0)),
        compiler_params=pltpu.CompilerParams(vmem_limit_bytes=32 * MIB),
        cost_estimate=pl.CostEstimate(
            flops=2 * rows * columns * window * sequences,
            bytes_accessed=4 * rows * columns + 2 * total_tok * (rows + columns),
            transcendentals=0,
        ),
    )(bounds, rot_grads, rot_inputs)


def attention(seq_ids, attn_weights, values):
    tok = values.shape[0]
    width = values.shape[1]
    heads = attn_weights.shape[1]
    window = attn_weights.shape[2]
    head_size = width // heads
    offset = lax.axis_index(("row", "col")) * tok
    previous = from_behind(values, ("row", "col"), 1)
    keys = jnp.concatenate([previous, values], axis=0).reshape(2 * tok, heads, head_size)
    query_pos = offset + jnp.arange(tok, dtype=jnp.int32)
    steps_back = jnp.arange(window, dtype=jnp.int32)
    query_seg = lax.dynamic_slice_in_dim(seq_ids, offset, tok, 0)
    run_start = jnp.sum((seq_ids[None, :] < query_seg[:, None]).astype(jnp.int32), axis=1)
    valid = (steps_back[None, :] <= (query_pos - run_start)[:, None]).astype(jnp.float32)
    masked = attn_weights * valid[:, None, :]
    probs = (masked / jnp.sum(masked, axis=2, keepdims=True)).astype(jnp.bfloat16)
    local_key = tok + jnp.arange(tok, dtype=jnp.int32)[:, None] - steps_back[None, :]
    selector = (
        local_key[:, :, None] == jnp.arange(2 * tok, dtype=jnp.int32)[None, None, :]
    ).astype(jnp.bfloat16)
    spread = jnp.einsum("phj,pjk->phk", probs, selector, preferred_element_type=jnp.float32).astype(
        jnp.bfloat16
    )
    mixed = jnp.einsum("phk,khd->phd", spread, keys, preferred_element_type=jnp.float32)
    return mixed.reshape(tok, width).astype(jnp.bfloat16)


MESH = pl.DeviceIdType.MESH


def merged(first, second):
    steps = [((i + 0.5) / len(first), 0, s) for i, s in enumerate(first)]
    steps += [((i + 0.5) / len(second), 1, s) for i, s in enumerate(second)]
    return [s for _, _, s in sorted(steps, key=lambda entry: entry[:2])]


def rotate_kernel(
    rows, cols, inputs_ref, grads_ref, act_hbm, grad_hbm, rot_grads_ref, rot_inputs_ref,
    grad_all, act_all, act_basis, grad_basis, part, pair, ring, rot_grads, act_part, down, up,
    local_sem, out_sem, a1_send, a1_recv, g1_send, g1_recv, a2_send, a2_recv, af_send, af_recv,
    g2_down, g2_up, g2_recv, pair_send, pair_recv, ring_send, ring_recv, ag_send, ag_recv,
    agf_send, agf_recv, down_send, down_recv, up_send, up_recv,
):
    chips = cols // 2
    tok = inputs_ref.shape[0]
    act_depth, act_width = act_basis.shape
    grad_depth, grad_width = grad_basis.shape
    r, c = lax.axis_index("row"), lax.axis_index("col")
    chip, core = c // 2, c % 2
    partner = (r, 2 * chip + 1 - core)
    not_last, not_first = r < rows - 1, r > 0
    pending = []

    def remote(src, dst, send, recv, device):
        return pltpu.make_async_remote_copy(
            src_ref=src, dst_ref=dst, send_sem=send, recv_sem=recv, device_id=device,
            device_id_type=MESH,
        )

    def send(copy, condition=None):
        pending.append((copy, condition))
        if condition is None:
            copy.start()
        else:
            pl.when(condition)(copy.start)

    def arrived(dst, recv, condition=None):
        copy = remote(dst, dst, recv, recv, partner)
        if condition is None:
            copy.wait_recv()
        else:
            pl.when(condition)(copy.wait_recv)

    load_grad = pltpu.make_async_copy(grad_hbm, grad_basis, local_sem.at[0])
    load_act = pltpu.make_async_copy(act_hbm, act_basis, local_sem.at[1])
    load_grad.start()
    load_act.start()

    other_rows = [(r + d) % rows for d in range(1, rows)]
    other_cols = [(c + d) % cols for d in range(1, cols)]
    other_chips = [(chip + d) % chips for d in range(1, chips)]
    barrier = pltpu.get_barrier_semaphore()
    for other in other_rows:
        pl.semaphore_signal(barrier, inc=1, device_id=(other, c), device_id_type=MESH)
    for other in other_cols:
        pl.semaphore_signal(barrier, inc=1, device_id=(r, other), device_id_type=MESH)
    pl.semaphore_wait(barrier, rows + cols - 2)

    def act_columns(row):
        return inputs_ref.at[:, pl.ds(pl.multiple_of(row * act_depth, act_depth), act_depth)]

    def grad_columns(col):
        return grads_ref.at[:, pl.ds(pl.multiple_of(col * grad_depth, grad_depth), grad_depth)]

    for other in other_rows:
        send(remote(act_columns(other), act_all.at[chip, core, r], a1_send.at[other],
                    a1_recv.at[r], (other, c)))
    for other in other_cols:
        send(remote(grad_columns(other), grad_all.at[r, chip, core], g1_send.at[other],
                    g1_recv.at[c], (r, other)))
    act_all[chip, core, r] = act_columns(r)[...]
    grad_all[r, chip, core] = grad_columns(c)[...]

    for other in other_rows:
        arrived(act_all.at[chip, core, other], a1_recv.at[other])
    for other in other_chips:
        send(remote(act_all.at[chip, core], act_all.at[chip, core], a2_send.at[other],
                    a2_recv.at[chip], (r, 2 * other + core)))
    send(remote(act_all.at[chip, core], act_all.at[chip, core], af_send.at[chip],
                af_recv.at[chip], partner))
    for other in other_cols:
        arrived(grad_all.at[r, other // 2, other % 2], g1_recv.at[other])

    order = [sorted(range(rows), key=lambda b: (abs(b - row), b)) for row in range(rows)]
    blocks = []
    for slot in range(rows):
        block = 0
        for row in range(rows):
            block = block + jnp.where(r == row, order[row][slot], 0)
        blocks.append(block)

    def grad_rotate(slot):
        block = blocks[slot]
        if slot > 0:
            arrived(grad_all.at[block], g2_recv.at[block])
        send(remote(grad_all.at[block], grad_all.at[block], g2_down.at[slot], g2_recv.at[block],
                    (jnp.minimum(r + 1, rows - 1), c)),
             jnp.logical_and(block <= r, not_last))
        send(remote(grad_all.at[block], grad_all.at[block], g2_up.at[slot], g2_recv.at[block],
                    (jnp.maximum(r - 1, 0), c)),
             jnp.logical_and(block >= r, not_first))
        if slot == 0:
            load_grad.wait()
        width = min(512, grad_width)

        @pl.loop(0, grad_width // width)
        def _(j):
            at = pl.ds(pl.multiple_of(j * width, width), width)
            term = jnp.dot(
                grad_all[block].reshape(cols * tok, grad_depth), grad_basis[:, at],
                preferred_element_type=jnp.float32,
            )
            part[block, :, :, :, at] = term.astype(jnp.bfloat16).reshape(chips, 2, tok, width)

        send(remote(part.at[block, :, 1 - core], pair.at[block], pair_send.at[slot],
                    pair_recv.at[block], partner))

    def grad_pair(slot):
        block = blocks[slot]
        arrived(pair.at[block], pair_recv.at[block])

        @pl.loop(0, chips)
        def _(k):
            total = part[block, k, core].astype(jnp.float32) + pair[block, k].astype(jnp.float32)
            part[block, k, core] = total.astype(jnp.bfloat16)

        for other in other_chips:
            send(remote(part.at[block, other, core], ring.at[block, chip],
                        ring_send.at[slot, other], ring_recv.at[block, chip],
                        (r, 2 * other + core)))

    def grad_sum(slot):
        block = blocks[slot]
        for other in other_chips:
            arrived(ring.at[block, other], ring_recv.at[block, other])
        width = min(512, grad_width)

        @pl.loop(0, grad_width // width)
        def _(j):
            at = pl.ds(pl.multiple_of(j * width, width), width)
            total = part[block, chip, core, :, at].astype(jnp.float32)
            for other in other_chips:
                total = total + ring[block, other, :, at].astype(jnp.float32)
            rot_grads[block, chip, core, :, at] = total.astype(jnp.bfloat16)

        for other in other_chips:
            send(remote(rot_grads.at[block, chip, core], rot_grads.at[block, chip, core],
                        ag_send.at[slot, other], ag_recv.at[block, chip],
                        (r, 2 * other + core)))

    def grad_share(slot):
        block = blocks[slot]
        for other in other_chips:
            arrived(rot_grads.at[block, other, core], ag_recv.at[block, other])
        send(remote(rot_grads.at[block, :, core], rot_grads.at[block, :, core],
                    agf_send.at[slot], agf_recv.at[block], partner))

    def grad_tick(tick):
        if tick < rows:
            grad_rotate(tick)
        if 0 <= tick - 1 < rows:
            grad_pair(tick - 1)
        if 0 <= tick - 2 < rows:
            grad_sum(tick - 2)
        if 0 <= tick - 3 < rows:
            grad_share(tick - 3)

    def act_rotate(step):
        k = (chip + step) % chips
        if step > 0:
            arrived(act_all.at[k, core], a2_recv.at[k])
            send(remote(act_all.at[k, core], act_all.at[k, core], af_send.at[k], af_recv.at[k],
                        partner))
        arrived(act_all.at[k, 1 - core], af_recv.at[k])
        if step == 0:
            load_act.wait()
        width = min(512, act_width)

        @pl.loop(0, act_width // width)
        def _(j):
            at = pl.ds(pl.multiple_of(j * width, width), width)
            term = jnp.dot(
                act_all[k].reshape(2 * rows * tok, act_depth), act_basis[:, at],
                preferred_element_type=jnp.float32,
            )
            act_part[k, :, :, :, at] = term.astype(jnp.bfloat16).reshape(2, rows, tok, width)

        @pl.when(r == 0)
        def _():
            down[k] = act_part[k]

        @pl.when(r == rows - 1)
        def _():
            up[k] = act_part[k]

        for half in range(2):
            send_down(k, half, r == 0)
            send_up(k, half, r == rows - 1)

    def send_down(k, half, condition):
        copy = remote(down.at[k, half], down.at[k, half], down_send.at[k, half],
                      down_recv.at[k, half], (jnp.minimum(r + 1, rows - 1), c))
        send(copy, condition)

    def send_up(k, half, condition):
        copy = remote(up.at[k, half], up.at[k, half], up_send.at[k, half],
                      up_recv.at[k, half], (jnp.maximum(r - 1, 0), c))
        send(copy, condition)

    stores = []

    def act_chain(step):
        k = (chip + step) % chips
        for half in range(2):
            @pl.when(not_first)
            def _():
                remote(down.at[k, half], down.at[k, half], down_send.at[k, half],
                       down_recv.at[k, half], partner).wait_recv()

                @pl.loop(0, rows)
                def _(q):
                    total = down[k, half, q].astype(jnp.float32)
                    total = total + act_part[k, half, q].astype(jnp.float32)
                    down[k, half, q] = total.astype(jnp.bfloat16)

            send_down(k, half, jnp.logical_and(not_first, not_last))

            @pl.when(not_last)
            def _():
                remote(up.at[k, half], up.at[k, half], up_send.at[k, half],
                       up_recv.at[k, half], partner).wait_recv()

                @pl.loop(0, rows)
                def _(q):
                    above = up[k, half, q].astype(jnp.float32)
                    own = act_part[k, half, q].astype(jnp.float32)
                    below = down[k, half, q].astype(jnp.float32)
                    up[k, half, q] = (above + own).astype(jnp.bfloat16)
                    act_part[k, half, q] = (above + below).astype(jnp.bfloat16)

            @pl.when(r == rows - 1)
            def _():
                act_part[k, half] = down[k, half]

            send_up(k, half, jnp.logical_and(not_first, not_last))
            store = pltpu.make_async_copy(
                act_part.at[k, half], rot_inputs_ref.at[:, k, half], out_sem.at[rows + 2 * step + half]
            )
            store.start()
            stores.append(store)

    ticks = [functools.partial(grad_tick, t) for t in range(rows + 3)]
    rotates = [functools.partial(act_rotate, s) for s in range(chips)]
    chains = [functools.partial(act_chain, s) for s in range(chips)]
    for step in merged(ticks[: rows - 1], rotates) + merged(chains, ticks[rows - 1 :]):
        step()
    for slot in range(rows):
        block = blocks[slot]
        arrived(rot_grads.at[block, :, 1 - core], agf_recv.at[block])
        store = pltpu.make_async_copy(rot_grads.at[block], rot_grads_ref.at[block], out_sem.at[slot])
        store.start()
        stores.append(store)
    for copy, condition in pending:
        if condition is None:
            copy.wait_send()
        else:
            pl.when(condition)(copy.wait_send)
    for store in stores:
        store.wait()


def rotate(inputs, out_grads, act_basis, grad_basis):
    rows, cols = lax.axis_size("row"), lax.axis_size("col")
    chips = cols // 2
    tok = inputs.shape[0]
    total_tok = rows * cols * tok
    act_depth, act_width = act_basis.shape
    grad_depth, grad_width = grad_basis.shape
    bf16 = jnp.bfloat16
    vmem, dma = pltpu.VMEM, pltpu.SemaphoreType.DMA
    rot_grads, rot_inputs = pl.pallas_call(
        functools.partial(rotate_kernel, rows, cols),
        out_shape=(
            jax.ShapeDtypeStruct((rows, chips, 2, tok, grad_width), bf16),
            jax.ShapeDtypeStruct((rows, chips, 2, tok, act_width), bf16),
        ),
        in_specs=[
            pl.BlockSpec(memory_space=pltpu.VMEM),
            pl.BlockSpec(memory_space=pltpu.VMEM),
            pl.BlockSpec(memory_space=pl.ANY),
            pl.BlockSpec(memory_space=pl.ANY),
        ],
        out_specs=(pl.BlockSpec(memory_space=pl.ANY), pl.BlockSpec(memory_space=pl.ANY)),
        scratch_shapes=[
            vmem((rows, chips, 2, tok, grad_depth), bf16),
            vmem((chips, 2, rows, tok, act_depth), bf16),
            vmem(act_basis.shape, bf16),
            vmem(grad_basis.shape, bf16),
            vmem((rows, chips, 2, tok, grad_width), bf16),
            vmem((rows, chips, tok, grad_width), bf16),
            vmem((rows, chips, tok, grad_width), bf16),
            vmem((rows, chips, 2, tok, grad_width), bf16),
            vmem((chips, 2, rows, tok, act_width), bf16),
            vmem((chips, 2, rows, tok, act_width), bf16),
            vmem((chips, 2, rows, tok, act_width), bf16),
            dma((2,)), dma((rows + cols,)),
            dma((rows,)), dma((rows,)), dma((cols,)), dma((cols,)),
            dma((chips,)), dma((chips,)), dma((chips,)), dma((chips,)),
            dma((rows,)), dma((rows,)), dma((rows,)),
            dma((rows,)), dma((rows,)),
            dma((rows, chips)), dma((rows, chips)), dma((rows, chips)), dma((rows, chips)),
            dma((rows,)), dma((rows,)),
            dma((chips, 2)), dma((chips, 2)), dma((chips, 2)), dma((chips, 2)),
        ],
        compiler_params=pltpu.CompilerParams(
            collective_id=0, has_side_effects=True, vmem_limit_bytes=58 * MIB
        ),
        cost_estimate=pl.CostEstimate(
            flops=2 * total_tok * (act_depth * act_width + grad_depth * grad_width),
            bytes_accessed=4 * (act_depth * act_width + grad_depth * grad_width),
            transcendentals=0,
        ),
    )(inputs, out_grads, act_basis, grad_basis)
    return rot_grads.reshape(total_tok, grad_width), rot_inputs.reshape(total_tok, act_width)


def shards(seq_ids, attn_weights, values, out_grads, act_basis, grad_basis):
    total_tok = seq_ids.shape[0]
    sequences = total_tok // SEQ_MEAN
    inputs = attention(seq_ids, attn_weights, values)
    rot_grads, rot_inputs = rotate(inputs, out_grads, act_basis, grad_basis)
    seq_range = jnp.arange(sequences + 1, dtype=jnp.int32)
    bounds = jnp.sum((seq_ids[None, :] < seq_range[:, None]).astype(jnp.int32), axis=1)
    return fit(bounds, rot_grads, rot_inputs, sequences)

def solution(mesh):
    return jax.shard_map(
        shards,
        mesh=mesh,
        in_specs=(
            P(),
            P(("row", "col"), None, None),
            P(("row", "col"), None),
            P(("row", "col"), None),
            P("row", "col"),
            P("col", "row"),
        ),
        out_specs=P("row", "col"),
        check_vma=False,
    )
```

```python
import functools
import jax
import jax.numpy as jnp
from jax import lax
from jax.experimental import pallas as pl
from jax.experimental.pallas import tpu as pltpu
from jax.sharding import PartitionSpec as P

SEQ_MEAN = 128
LONGEST = 192
MIB = 1 << 20


def from_behind(value, axis, steps):
    count = lax.axis_size(axis)
    initial, last = (max(0, -steps), min(count, count - steps))
    return lax.ppermute(value, axis, [(source, source + steps) for source in range(initial, last)])


def fit_kernel(sequences, window, bounds_ref, grads_ref, acts_ref, out_ref):
    total_tok = grads_ref.shape[0]
    positions = lax.broadcasted_iota(jnp.int32, (window, 1), 0)

    def tile(index):
        start, end = bounds_ref[index], bounds_ref[index + 1]
        first = pl.multiple_of(jnp.minimum(start // 16 * 16, total_tok - window), 16)
        here = positions + first
        inside = jnp.logical_and(here >= start, here < end)
        grads = grads_ref[pl.ds(first, window), :]
        grads = jnp.where(inside, grads, jnp.zeros_like(grads))
        acts = acts_ref[pl.ds(first, window), :]
        product = lax.dot_general(
            grads, acts, (((0,), (0,)), ((), ())), preferred_element_type=jnp.float32
        )
        return product * product

    group = 4

    def squares(index):
        total = tile(index)
        for step in range(1, group):
            total = total + tile(index + step)
        return total

    out_ref[...] = squares(0)

    @pl.loop(1, sequences // group - 1)
    def _(index):
        out_ref[...] += squares(index * group)

    out_ref[...] = (out_ref[...] + squares(sequences - group)) * (1.0 / sequences)


def fit(bounds, rot_grads, rot_inputs, sequences):
    total_tok, rows = rot_grads.shape
    columns = rot_inputs.shape[1]
    height = 256
    window = (LONGEST + 15 + 127) // 128 * 128
    return pl.pallas_call(
        functools.partial(fit_kernel, sequences, window),
        grid=(rows // height,),
        out_shape=jax.ShapeDtypeStruct((rows, columns), jnp.float32),
        in_specs=[
            pl.BlockSpec(memory_space=pltpu.SMEM),
            pl.BlockSpec((total_tok, height), lambda i: (0, i)),
            pl.BlockSpec((total_tok, columns), lambda i: (0, 0)),
        ],
        out_specs=pl.BlockSpec((height, columns), lambda i: (i, 0)),
        compiler_params=pltpu.CompilerParams(vmem_limit_bytes=32 * MIB),
        cost_estimate=pl.CostEstimate(
            flops=2 * rows * columns * window * sequences,
            bytes_accessed=4 * rows * columns + 2 * total_tok * (rows + columns),
            transcendentals=0,
        ),
    )(bounds, rot_grads, rot_inputs)


def attention(seq_ids, attn_weights, values):
    tok = values.shape[0]
    width = values.shape[1]
    heads = attn_weights.shape[1]
    window = attn_weights.shape[2]
    head_size = width // heads
    offset = lax.axis_index(("row", "col")) * tok
    previous = from_behind(values, ("row", "col"), 1)
    keys = jnp.concatenate([previous, values], axis=0).reshape(2 * tok, heads, head_size)
    query_pos = offset + jnp.arange(tok, dtype=jnp.int32)
    steps_back = jnp.arange(window, dtype=jnp.int32)
    query_seg = lax.dynamic_slice_in_dim(seq_ids, offset, tok, 0)
    run_start = jnp.sum((seq_ids[None, :] < query_seg[:, None]).astype(jnp.int32), axis=1)
    valid = (steps_back[None, :] <= (query_pos - run_start)[:, None]).astype(jnp.float32)
    masked = attn_weights * valid[:, None, :]
    probs = (masked / jnp.sum(masked, axis=2, keepdims=True)).astype(jnp.bfloat16)
    local_key = tok + jnp.arange(tok, dtype=jnp.int32)[:, None] - steps_back[None, :]
    selector = (
        local_key[:, :, None] == jnp.arange(2 * tok, dtype=jnp.int32)[None, None, :]
    ).astype(jnp.bfloat16)
    spread = jnp.einsum("phj,pjk->phk", probs, selector, preferred_element_type=jnp.float32).astype(
        jnp.bfloat16
    )
    mixed = jnp.einsum("phk,khd->phd", spread, keys, preferred_element_type=jnp.float32)
    return mixed.reshape(tok, width).astype(jnp.bfloat16)


MESH = pl.DeviceIdType.MESH


def merged(first, second):
    steps = [((i + 0.5) / len(first), 0, s) for i, s in enumerate(first)]
    steps += [((i + 0.5) / len(second), 1, s) for i, s in enumerate(second)]
    return [s for _, _, s in sorted(steps, key=lambda entry: entry[:2])]


def rotate_kernel(
    rows, cols, inputs_ref, grads_ref, act_hbm, grad_hbm, rot_grads_ref, rot_inputs_ref,
    grad_all, act_all, act_basis, grad_basis, part, pair, ring, rot_grads, act_part, down, up,
    local_sem, out_sem, a1_send, a1_recv, g1_send, g1_recv, a2_send, a2_recv, af_send, af_recv,
    g2_down, g2_up, g2_recv, pair_send, pair_recv, ring_send, ring_recv, ag_send, ag_recv,
    agf_send, agf_recv, down_send, down_recv, up_send, up_recv,
):
    chips = cols // 2
    tok = inputs_ref.shape[0]
    act_depth, act_width = act_basis.shape
    grad_depth, grad_width = grad_basis.shape
    r, c = lax.axis_index("row"), lax.axis_index("col")
    chip, core = c // 2, c % 2
    partner = (r, 2 * chip + 1 - core)
    not_last, not_first = r < rows - 1, r > 0
    pending = []

    def remote(src, dst, send, recv, device):
        return pltpu.make_async_remote_copy(
            src_ref=src, dst_ref=dst, send_sem=send, recv_sem=recv, device_id=device,
            device_id_type=MESH,
        )

    def send(copy, condition=None):
        pending.append((copy, condition))
        if condition is None:
            copy.start()
        else:
            pl.when(condition)(copy.start)

    def arrived(dst, recv, condition=None):
        copy = remote(dst, dst, recv, recv, partner)
        if condition is None:
            copy.wait_recv()
        else:
            pl.when(condition)(copy.wait_recv)

    load_grad = pltpu.make_async_copy(grad_hbm, grad_basis, local_sem.at[0])
    load_act = pltpu.make_async_copy(act_hbm, act_basis, local_sem.at[1])
    load_grad.start()
    load_act.start()

    other_rows = [(r + d) % rows for d in range(1, rows)]
    other_cols = [(c + d) % cols for d in range(1, cols)]
    other_chips = [(chip + d) % chips for d in range(1, chips)]
    barrier = pltpu.get_barrier_semaphore()
    for other in other_rows:
        pl.semaphore_signal(barrier, inc=1, device_id=(other, c), device_id_type=MESH)
    for other in other_cols:
        pl.semaphore_signal(barrier, inc=1, device_id=(r, other), device_id_type=MESH)
    pl.semaphore_wait(barrier, rows + cols - 2)

    def act_columns(row):
        return inputs_ref.at[:, pl.ds(pl.multiple_of(row * act_depth, act_depth), act_depth)]

    def grad_columns(col):
        return grads_ref.at[:, pl.ds(pl.multiple_of(col * grad_depth, grad_depth), grad_depth)]

    for other in other_rows:
        send(remote(act_columns(other), act_all.at[chip, core, r], a1_send.at[other],
                    a1_recv.at[r], (other, c)))
    for other in other_cols:
        send(remote(grad_columns(other), grad_all.at[r, chip, core], g1_send.at[other],
                    g1_recv.at[c], (r, other)))
    act_all[chip, core, r] = act_columns(r)[...]
    grad_all[r, chip, core] = grad_columns(c)[...]

    for other in other_rows:
        arrived(act_all.at[chip, core, other], a1_recv.at[other])
    for other in other_chips:
        send(remote(act_all.at[chip, core], act_all.at[chip, core], a2_send.at[other],
                    a2_recv.at[chip], (r, 2 * other + core)))
    send(remote(act_all.at[chip, core], act_all.at[chip, core], af_send.at[chip],
                af_recv.at[chip], partner))
    for other in other_cols:
        arrived(grad_all.at[r, other // 2, other % 2], g1_recv.at[other])

    order = [sorted(range(rows), key=lambda b: (abs(b - row), b)) for row in range(rows)]
    blocks = []
    for slot in range(rows):
        block = 0
        for row in range(rows):
            block = block + jnp.where(r == row, order[row][slot], 0)
        blocks.append(block)

    def grad_rotate(slot):
        block = blocks[slot]
        if slot > 0:
            arrived(grad_all.at[block], g2_recv.at[block])
        send(remote(grad_all.at[block], grad_all.at[block], g2_down.at[slot], g2_recv.at[block],
                    (jnp.minimum(r + 1, rows - 1), c)),
             jnp.logical_and(block <= r, not_last))
        send(remote(grad_all.at[block], grad_all.at[block], g2_up.at[slot], g2_recv.at[block],
                    (jnp.maximum(r - 1, 0), c)),
             jnp.logical_and(block >= r, not_first))
        if slot == 0:
            load_grad.wait()
        width = min(512, grad_width)

        @pl.loop(0, grad_width // width)
        def _(j):
            at = pl.ds(pl.multiple_of(j * width, width), width)
            term = jnp.dot(
                grad_all[block].reshape(cols * tok, grad_depth), grad_basis[:, at],
                preferred_element_type=jnp.float32,
            )
            part[block, :, :, :, at] = term.astype(jnp.bfloat16).reshape(chips, 2, tok, width)

        send(remote(part.at[block, :, 1 - core], pair.at[block], pair_send.at[slot],
                    pair_recv.at[block], partner))

    def grad_pair(slot):
        block = blocks[slot]
        arrived(pair.at[block], pair_recv.at[block])

        @pl.loop(0, chips)
        def _(k):
            total = part[block, k, core].astype(jnp.float32) + pair[block, k].astype(jnp.float32)
            part[block, k, core] = total.astype(jnp.bfloat16)

        for other in other_chips:
            send(remote(part.at[block, other, core], ring.at[block, chip],
                        ring_send.at[slot, other], ring_recv.at[block, chip],
                        (r, 2 * other + core)))

    def grad_sum(slot):
        block = blocks[slot]
        for other in other_chips:
            arrived(ring.at[block, other], ring_recv.at[block, other])
        width = min(512, grad_width)

        @pl.loop(0, grad_width // width)
        def _(j):
            at = pl.ds(pl.multiple_of(j * width, width), width)
            total = part[block, chip, core, :, at].astype(jnp.float32)
            for other in other_chips:
                total = total + ring[block, other, :, at].astype(jnp.float32)
            rot_grads[block, chip, core, :, at] = total.astype(jnp.bfloat16)

        for other in other_chips:
            send(remote(rot_grads.at[block, chip, core], rot_grads.at[block, chip, core],
                        ag_send.at[slot, other], ag_recv.at[block, chip],
                        (r, 2 * other + core)))

    def grad_share(slot):
        block = blocks[slot]
        for other in other_chips:
            arrived(rot_grads.at[block, other, core], ag_recv.at[block, other])
        send(remote(rot_grads.at[block, :, core], rot_grads.at[block, :, core],
                    agf_send.at[slot], agf_recv.at[block], partner))

    def grad_tick(tick):
        if tick < rows:
            grad_rotate(tick)
        if 0 <= tick - 1 < rows:
            grad_pair(tick - 1)
        if 0 <= tick - 2 < rows:
            grad_sum(tick - 2)
        if 0 <= tick - 3 < rows:
            grad_share(tick - 3)

    def act_rotate(step):
        k = (chip + step) % chips
        if step > 0:
            arrived(act_all.at[k, core], a2_recv.at[k])
            send(remote(act_all.at[k, core], act_all.at[k, core], af_send.at[k], af_recv.at[k],
                        partner))
        arrived(act_all.at[k, 1 - core], af_recv.at[k])
        if step == 0:
            load_act.wait()
        width = min(512, act_width)

        @pl.loop(0, act_width // width)
        def _(j):
            at = pl.ds(pl.multiple_of(j * width, width), width)
            term = jnp.dot(
                act_all[k].reshape(2 * rows * tok, act_depth), act_basis[:, at],
                preferred_element_type=jnp.float32,
            )
            act_part[k, :, :, :, at] = term.astype(jnp.bfloat16).reshape(2, rows, tok, width)

        @pl.when(r == 0)
        def _():
            down[k] = act_part[k]

        @pl.when(r == rows - 1)
        def _():
            up[k] = act_part[k]

        for half in range(2):
            pl.when(r == 0)(down_copy(k, half).start)
            pl.when(r == rows - 1)(up_copy(k, half).start)

    def down_copy(k, half):
        return remote(down.at[k, half], down.at[k, half], down_send.at[k, half],
                      down_recv.at[k, half], (jnp.minimum(r + 1, rows - 1), c))

    def up_copy(k, half):
        return remote(up.at[k, half], up.at[k, half], up_send.at[k, half],
                      up_recv.at[k, half], (jnp.maximum(r - 1, 0), c))

    def result_copy(k, half):
        return pltpu.make_async_copy(
            act_part.at[k, half], rot_inputs_ref.at[:, k, half], out_sem.at[rows + 2 * k + half]
        )

    def chain_step(flow, other, copy, index, has_next, is_second):
        k, half = (chip + index // 2) % chips, index % 2
        copy(k, half).wait_recv()

        @pl.when(is_second)
        def _():
            @pl.loop(0, rows)
            def _(q):
                before = flow[k, half, q].astype(jnp.float32)
                own = act_part[k, half, q].astype(jnp.float32)
                rest = other[k, half, q].astype(jnp.float32)
                flow[k, half, q] = (before + own).astype(jnp.bfloat16)
                act_part[k, half, q] = (before + rest).astype(jnp.bfloat16)

        @pl.when(jnp.logical_not(is_second))
        def _():
            @pl.loop(0, rows)
            def _(q):
                before = flow[k, half, q].astype(jnp.float32)
                own = act_part[k, half, q].astype(jnp.float32)
                flow[k, half, q] = (before + own).astype(jnp.bfloat16)

        pl.when(has_next)(copy(k, half).start)
        pl.when(is_second)(result_copy(k, half).start)

    upper = 2 * r >= rows

    def act_chain(time):
        below, above = time - r, time - (rows - 1 - r)

        @pl.when(jnp.logical_and(not_first, jnp.logical_and(below >= 0, below < cols)))
        def _():
            chain_step(down, up, down_copy, below, not_last, upper)

        @pl.when(jnp.logical_and(not_last, jnp.logical_and(above >= 0, above < cols)))
        def _():
            chain_step(up, down, up_copy, above, not_first, jnp.logical_not(upper))

    stores = []
    ticks = [functools.partial(grad_tick, t) for t in range(rows + 3)]
    rotates = [functools.partial(act_rotate, s) for s in range(chips)]
    chains = [functools.partial(act_chain, t) for t in range(1, cols + rows - 1)]
    early = rows // 2
    for step in merged(ticks[:early], rotates[:-1]) + rotates[-1:] + merged(chains, ticks[early:]):
        step()
    for slot in range(rows):
        block = blocks[slot]
        arrived(rot_grads.at[block, :, 1 - core], agf_recv.at[block])
        store = pltpu.make_async_copy(rot_grads.at[block], rot_grads_ref.at[block], out_sem.at[slot])
        store.start()
        stores.append(store)
    for copy, condition in pending:
        if condition is None:
            copy.wait_send()
        else:
            pl.when(condition)(copy.wait_send)
    for k in range(chips):
        for half in range(2):
            pl.when(not_last)(down_copy(k, half).wait_send)
            pl.when(not_first)(up_copy(k, half).wait_send)
            result_copy(k, half).wait()
    for store in stores:
        store.wait()


def rotate(inputs, out_grads, act_basis, grad_basis):
    rows, cols = lax.axis_size("row"), lax.axis_size("col")
    chips = cols // 2
    tok = inputs.shape[0]
    total_tok = rows * cols * tok
    act_depth, act_width = act_basis.shape
    grad_depth, grad_width = grad_basis.shape
    bf16 = jnp.bfloat16
    vmem, dma = pltpu.VMEM, pltpu.SemaphoreType.DMA
    rot_grads, rot_inputs = pl.pallas_call(
        functools.partial(rotate_kernel, rows, cols),
        out_shape=(
            jax.ShapeDtypeStruct((rows, chips, 2, tok, grad_width), bf16),
            jax.ShapeDtypeStruct((rows, chips, 2, tok, act_width), bf16),
        ),
        in_specs=[
            pl.BlockSpec(memory_space=pltpu.VMEM),
            pl.BlockSpec(memory_space=pltpu.VMEM),
            pl.BlockSpec(memory_space=pl.ANY),
            pl.BlockSpec(memory_space=pl.ANY),
        ],
        out_specs=(pl.BlockSpec(memory_space=pl.ANY), pl.BlockSpec(memory_space=pl.ANY)),
        scratch_shapes=[
            vmem((rows, chips, 2, tok, grad_depth), bf16),
            vmem((chips, 2, rows, tok, act_depth), bf16),
            vmem(act_basis.shape, bf16),
            vmem(grad_basis.shape, bf16),
            vmem((rows, chips, 2, tok, grad_width), bf16),
            vmem((rows, chips, tok, grad_width), bf16),
            vmem((rows, chips, tok, grad_width), bf16),
            vmem((rows, chips, 2, tok, grad_width), bf16),
            vmem((chips, 2, rows, tok, act_width), bf16),
            vmem((chips, 2, rows, tok, act_width), bf16),
            vmem((chips, 2, rows, tok, act_width), bf16),
            dma((2,)), dma((rows + cols,)),
            dma((rows,)), dma((rows,)), dma((cols,)), dma((cols,)),
            dma((chips,)), dma((chips,)), dma((chips,)), dma((chips,)),
            dma((rows,)), dma((rows,)), dma((rows,)),
            dma((rows,)), dma((rows,)),
            dma((rows, chips)), dma((rows, chips)), dma((rows, chips)), dma((rows, chips)),
            dma((rows,)), dma((rows,)),
            dma((chips, 2)), dma((chips, 2)), dma((chips, 2)), dma((chips, 2)),
        ],
        compiler_params=pltpu.CompilerParams(
            collective_id=0, has_side_effects=True, vmem_limit_bytes=58 * MIB
        ),
        cost_estimate=pl.CostEstimate(
            flops=2 * total_tok * (act_depth * act_width + grad_depth * grad_width),
            bytes_accessed=4 * (act_depth * act_width + grad_depth * grad_width),
            transcendentals=0,
        ),
    )(inputs, out_grads, act_basis, grad_basis)
    return rot_grads.reshape(total_tok, grad_width), rot_inputs.reshape(total_tok, act_width)


def shards(seq_ids, attn_weights, values, out_grads, act_basis, grad_basis):
    total_tok = seq_ids.shape[0]
    sequences = total_tok // SEQ_MEAN
    inputs = attention(seq_ids, attn_weights, values)
    rot_grads, rot_inputs = rotate(inputs, out_grads, act_basis, grad_basis)
    seq_range = jnp.arange(sequences + 1, dtype=jnp.int32)
    bounds = jnp.sum((seq_ids[None, :] < seq_range[:, None]).astype(jnp.int32), axis=1)
    return fit(bounds, rot_grads, rot_inputs, sequences)

def solution(mesh):
    return jax.shard_map(
        shards,
        mesh=mesh,
        in_specs=(
            P(),
            P(("row", "col"), None, None),
            P(("row", "col"), None),
            P(("row", "col"), None),
            P("row", "col"),
            P("col", "row"),
        ),
        out_specs=P("row", "col"),
        check_vma=False,
    )
```

```python
import functools
import jax
import jax.numpy as jnp
from jax import lax
from jax.experimental import pallas as pl
from jax.experimental.pallas import tpu as pltpu
from jax.sharding import PartitionSpec as P

SEQ_MEAN = 128
LONGEST = 192
MIB = 1 << 20


def from_behind(value, axis, steps):
    count = lax.axis_size(axis)
    initial, last = (max(0, -steps), min(count, count - steps))
    return lax.ppermute(value, axis, [(source, source + steps) for source in range(initial, last)])


def fit_kernel(sequences, window, bounds_ref, grads_ref, acts_ref, out_ref):
    total_tok = grads_ref.shape[0]
    positions = lax.broadcasted_iota(jnp.int32, (window, 1), 0)

    def tile(index):
        start, end = bounds_ref[index], bounds_ref[index + 1]
        first = pl.multiple_of(jnp.minimum(start // 16 * 16, total_tok - window), 16)
        here = positions + first
        inside = jnp.logical_and(here >= start, here < end)
        grads = grads_ref[pl.ds(first, window), :]
        grads = jnp.where(inside, grads, jnp.zeros_like(grads))
        acts = acts_ref[pl.ds(first, window), :]
        product = lax.dot_general(
            grads, acts, (((0,), (0,)), ((), ())), preferred_element_type=jnp.float32
        )
        return product * product

    group = 4

    def squares(index):
        total = tile(index)
        for step in range(1, group):
            total = total + tile(index + step)
        return total

    out_ref[...] = squares(0)

    @pl.loop(1, sequences // group - 1)
    def _(index):
        out_ref[...] += squares(index * group)

    out_ref[...] = (out_ref[...] + squares(sequences - group)) * (1.0 / sequences)


def fit(bounds, rot_grads, rot_inputs, sequences):
    total_tok, rows = rot_grads.shape
    columns = rot_inputs.shape[1]
    height = 256
    window = (LONGEST + 15 + 127) // 128 * 128
    return pl.pallas_call(
        functools.partial(fit_kernel, sequences, window),
        grid=(rows // height,),
        out_shape=jax.ShapeDtypeStruct((rows, columns), jnp.float32),
        in_specs=[
            pl.BlockSpec(memory_space=pltpu.SMEM),
            pl.BlockSpec((total_tok, height), lambda i: (0, i)),
            pl.BlockSpec((total_tok, columns), lambda i: (0, 0)),
        ],
        out_specs=pl.BlockSpec((height, columns), lambda i: (i, 0)),
        compiler_params=pltpu.CompilerParams(vmem_limit_bytes=58 * MIB),
        cost_estimate=pl.CostEstimate(
            flops=2 * rows * columns * window * sequences,
            bytes_accessed=4 * rows * columns + 2 * total_tok * (rows + columns),
            transcendentals=0,
        ),
    )(bounds, rot_grads, rot_inputs)


def attention(seq_ids, attn_weights, values):
    tok = values.shape[0]
    width = values.shape[1]
    heads = attn_weights.shape[1]
    window = attn_weights.shape[2]
    head_size = width // heads
    offset = lax.axis_index(("row", "col")) * tok
    previous = from_behind(values, ("row", "col"), 1)
    keys = jnp.concatenate([previous, values], axis=0).reshape(2 * tok, heads, head_size)
    query_pos = offset + jnp.arange(tok, dtype=jnp.int32)
    steps_back = jnp.arange(window, dtype=jnp.int32)
    query_seg = lax.dynamic_slice_in_dim(seq_ids, offset, tok, 0)
    run_start = jnp.sum((seq_ids[None, :] < query_seg[:, None]).astype(jnp.int32), axis=1)
    valid = (steps_back[None, :] <= (query_pos - run_start)[:, None]).astype(jnp.float32)
    masked = attn_weights * valid[:, None, :]
    probs = (masked / jnp.sum(masked, axis=2, keepdims=True)).astype(jnp.bfloat16)
    local_key = tok + jnp.arange(tok, dtype=jnp.int32)[:, None] - steps_back[None, :]
    selector = (
        local_key[:, :, None] == jnp.arange(2 * tok, dtype=jnp.int32)[None, None, :]
    ).astype(jnp.bfloat16)
    spread = jnp.einsum("phj,pjk->phk", probs, selector, preferred_element_type=jnp.float32).astype(
        jnp.bfloat16
    )
    mixed = jnp.einsum("phk,khd->phd", spread, keys, preferred_element_type=jnp.float32)
    return mixed.reshape(tok, width).astype(jnp.bfloat16)


MESH = pl.DeviceIdType.MESH


def merged(first, second):
    steps = [((i + 0.5) / len(first), 0, s) for i, s in enumerate(first)]
    steps += [((i + 0.5) / len(second), 1, s) for i, s in enumerate(second)]
    return [s for _, _, s in sorted(steps, key=lambda entry: entry[:2])]


def rotate_kernel(
    rows, cols, inputs_ref, grads_ref, act_hbm, grad_hbm, rot_grads_ref, rot_inputs_ref,
    grad_all, act_all, act_basis, grad_basis, part, pair, ring, rot_grads, act_part, down, up,
    local_sem, out_sem, a1_send, a1_recv, g1_send, g1_recv, a2_send, a2_recv, af_send, af_recv,
    g2_down, g2_up, g2_recv, pair_send, pair_recv, ring_send, ring_recv, ag_send, ag_recv,
    agf_send, agf_recv, down_send, down_recv, up_send, up_recv,
):
    chips = cols // 2
    tok = inputs_ref.shape[0]
    act_depth, act_width = act_basis.shape
    grad_depth, grad_width = grad_basis.shape
    r, c = lax.axis_index("row"), lax.axis_index("col")
    chip, core = c // 2, c % 2
    partner = (r, 2 * chip + 1 - core)
    not_last, not_first = r < rows - 1, r > 0
    pending = []

    def remote(src, dst, send, recv, device):
        return pltpu.make_async_remote_copy(
            src_ref=src, dst_ref=dst, send_sem=send, recv_sem=recv, device_id=device,
            device_id_type=MESH,
        )

    def send(copy, condition=None):
        pending.append((copy, condition))
        if condition is None:
            copy.start()
        else:
            pl.when(condition)(copy.start)

    def arrived(dst, recv, condition=None):
        copy = remote(dst, dst, recv, recv, partner)
        if condition is None:
            copy.wait_recv()
        else:
            pl.when(condition)(copy.wait_recv)

    load_grad = pltpu.make_async_copy(grad_hbm, grad_basis, local_sem.at[0])
    load_act = pltpu.make_async_copy(act_hbm, act_basis, local_sem.at[1])
    load_grad.start()
    load_act.start()

    other_rows = [(r + d) % rows for d in range(1, rows)]
    other_cols = [(c + d) % cols for d in range(1, cols)]
    other_chips = [(chip + d) % chips for d in range(1, chips)]
    barrier = pltpu.get_barrier_semaphore()
    for other in other_rows:
        pl.semaphore_signal(barrier, inc=1, device_id=(other, c), device_id_type=MESH)
    for other in other_cols:
        pl.semaphore_signal(barrier, inc=1, device_id=(r, other), device_id_type=MESH)
    pl.semaphore_wait(barrier, rows + cols - 2)

    def act_columns(row):
        return inputs_ref.at[:, pl.ds(pl.multiple_of(row * act_depth, act_depth), act_depth)]

    def grad_columns(col):
        return grads_ref.at[:, pl.ds(pl.multiple_of(col * grad_depth, grad_depth), grad_depth)]

    for other in other_rows:
        send(remote(act_columns(other), act_all.at[chip, core, r], a1_send.at[other],
                    a1_recv.at[r], (other, c)))
    for other in other_cols:
        send(remote(grad_columns(other), grad_all.at[r, chip, core], g1_send.at[other],
                    g1_recv.at[c], (r, other)))
    act_all[chip, core, r] = act_columns(r)[...]
    grad_all[r, chip, core] = grad_columns(c)[...]

    for other in other_rows:
        arrived(act_all.at[chip, core, other], a1_recv.at[other])
    for other in other_chips:
        send(remote(act_all.at[chip, core], act_all.at[chip, core], a2_send.at[other],
                    a2_recv.at[chip], (r, 2 * other + core)))
    send(remote(act_all.at[chip, core], act_all.at[chip, core], af_send.at[chip],
                af_recv.at[chip], partner))
    for other in other_cols:
        arrived(grad_all.at[r, other // 2, other % 2], g1_recv.at[other])

    order = [sorted(range(rows), key=lambda b: (abs(b - row), b)) for row in range(rows)]
    blocks = []
    for slot in range(rows):
        block = 0
        for row in range(rows):
            block = block + jnp.where(r == row, order[row][slot], 0)
        blocks.append(block)

    def grad_rotate(slot):
        block = blocks[slot]
        if slot > 0:
            arrived(grad_all.at[block], g2_recv.at[block])
        send(remote(grad_all.at[block], grad_all.at[block], g2_down.at[slot], g2_recv.at[block],
                    (jnp.minimum(r + 1, rows - 1), c)),
             jnp.logical_and(block <= r, not_last))
        send(remote(grad_all.at[block], grad_all.at[block], g2_up.at[slot], g2_recv.at[block],
                    (jnp.maximum(r - 1, 0), c)),
             jnp.logical_and(block >= r, not_first))
        if slot == 0:
            load_grad.wait()
        width = min(512, grad_width)

        @pl.loop(0, grad_width // width)
        def _(j):
            at = pl.ds(pl.multiple_of(j * width, width), width)
            term = jnp.dot(
                grad_all[block].reshape(cols * tok, grad_depth), grad_basis[:, at],
                preferred_element_type=jnp.float32,
            )
            part[block, :, :, :, at] = term.astype(jnp.bfloat16).reshape(chips, 2, tok, width)

        send(remote(part.at[block, :, 1 - core], pair.at[block], pair_send.at[slot],
                    pair_recv.at[block], partner))

    def grad_pair(slot):
        block = blocks[slot]
        arrived(pair.at[block], pair_recv.at[block])

        @pl.loop(0, chips)
        def _(k):
            total = part[block, k, core].astype(jnp.float32) + pair[block, k].astype(jnp.float32)
            part[block, k, core] = total.astype(jnp.bfloat16)

        for other in other_chips:
            send(remote(part.at[block, other, core], ring.at[block, chip],
                        ring_send.at[slot, other], ring_recv.at[block, chip],
                        (r, 2 * other + core)))

    def grad_sum(slot):
        block = blocks[slot]
        for other in other_chips:
            arrived(ring.at[block, other], ring_recv.at[block, other])
        width = min(512, grad_width)

        @pl.loop(0, grad_width // width)
        def _(j):
            at = pl.ds(pl.multiple_of(j * width, width), width)
            total = part[block, chip, core, :, at].astype(jnp.float32)
            for other in other_chips:
                total = total + ring[block, other, :, at].astype(jnp.float32)
            rot_grads[block, chip, core, :, at] = total.astype(jnp.bfloat16)

        for other in other_chips:
            send(remote(rot_grads.at[block, chip, core], rot_grads.at[block, chip, core],
                        ag_send.at[slot, other], ag_recv.at[block, chip],
                        (r, 2 * other + core)))

    def grad_share(slot):
        block = blocks[slot]
        for other in other_chips:
            arrived(rot_grads.at[block, other, core], ag_recv.at[block, other])
        send(remote(rot_grads.at[block, :, core], rot_grads.at[block, :, core],
                    agf_send.at[slot], agf_recv.at[block], partner))

    def grad_tick(tick):
        if tick < rows:
            grad_rotate(tick)
        if 0 <= tick - 1 < rows:
            grad_pair(tick - 1)
        if 0 <= tick - 2 < rows:
            grad_sum(tick - 2)
        if 0 <= tick - 3 < rows:
            grad_share(tick - 3)

    def act_rotate(step):
        k = (chip + step) % chips
        if step > 0:
            arrived(act_all.at[k, core], a2_recv.at[k])
            send(remote(act_all.at[k, core], act_all.at[k, core], af_send.at[k], af_recv.at[k],
                        partner))
        arrived(act_all.at[k, 1 - core], af_recv.at[k])
        if step == 0:
            load_act.wait()
        width = min(512, act_width)

        @pl.loop(0, act_width // width)
        def _(j):
            at = pl.ds(pl.multiple_of(j * width, width), width)
            term = jnp.dot(
                act_all[k].reshape(2 * rows * tok, act_depth), act_basis[:, at],
                preferred_element_type=jnp.float32,
            )
            act_part[k, :, :, :, at] = term.astype(jnp.bfloat16).reshape(2, rows, tok, width)

        @pl.when(r == 0)
        def _():
            down[k] = act_part[k]

        @pl.when(r == rows - 1)
        def _():
            up[k] = act_part[k]

        for index in range(2 * pieces):
            pl.when(r == 0)(down_copy(k, index).start)
            pl.when(r == rows - 1)(up_copy(k, index).start)

    pieces = 2
    span = rows // pieces

    def piece(ref, k, index):
        return ref.at[k, index // pieces, pl.ds(index % pieces * span, span)]

    def down_copy(k, index):
        return remote(piece(down, k, index), piece(down, k, index), down_send.at[k, index],
                      down_recv.at[k, index], (jnp.minimum(r + 1, rows - 1), c))

    def up_copy(k, index):
        return remote(piece(up, k, index), piece(up, k, index), up_send.at[k, index],
                      up_recv.at[k, index], (jnp.maximum(r - 1, 0), c))

    def result_copy(k, index):
        return pltpu.make_async_copy(
            piece(act_part, k, index),
            rot_inputs_ref.at[pl.ds(index % pieces * span, span), k, index // pieces],
            out_sem.at[rows + 2 * pieces * k + index],
        )

    def chain_step(flow, other, copy, number, has_next, is_second):
        k, index = (chip + number // (2 * pieces)) % chips, number % (2 * pieces)
        half, first = index // pieces, index % pieces * span
        copy(k, index).wait_recv()

        @pl.when(is_second)
        def _():
            @pl.loop(0, span)
            def _(step):
                q = first + step
                before = flow[k, half, q].astype(jnp.float32)
                own = act_part[k, half, q].astype(jnp.float32)
                rest = other[k, half, q].astype(jnp.float32)
                flow[k, half, q] = (before + own).astype(jnp.bfloat16)
                act_part[k, half, q] = (before + rest).astype(jnp.bfloat16)

        @pl.when(jnp.logical_not(is_second))
        def _():
            @pl.loop(0, span)
            def _(step):
                q = first + step
                before = flow[k, half, q].astype(jnp.float32)
                own = act_part[k, half, q].astype(jnp.float32)
                flow[k, half, q] = (before + own).astype(jnp.bfloat16)

        pl.when(has_next)(copy(k, index).start)
        pl.when(is_second)(result_copy(k, index).start)

    upper = 2 * r >= rows

    def act_chain(time):
        below, above = time - r, time - (rows - 1 - r)

        @pl.when(jnp.logical_and(not_first, jnp.logical_and(below >= 0, below < cols * pieces)))
        def _():
            chain_step(down, up, down_copy, below, not_last, upper)

        @pl.when(jnp.logical_and(not_last, jnp.logical_and(above >= 0, above < cols * pieces)))
        def _():
            chain_step(up, down, up_copy, above, not_first, jnp.logical_not(upper))

    stores = []
    ticks = [functools.partial(grad_tick, t) for t in range(rows + 3)]
    rotates = [functools.partial(act_rotate, s) for s in range(chips)]
    chains = [functools.partial(act_chain, t) for t in range(1, cols * pieces + rows - 1)]
    early = rows // 2
    for step in merged(ticks[:early], rotates[:-1]) + rotates[-1:] + merged(chains, ticks[early:]):
        step()
    for slot in range(rows):
        block = blocks[slot]
        arrived(rot_grads.at[block, :, 1 - core], agf_recv.at[block])
        store = pltpu.make_async_copy(rot_grads.at[block], rot_grads_ref.at[block], out_sem.at[slot])
        store.start()
        stores.append(store)
    for copy, condition in pending:
        if condition is None:
            copy.wait_send()
        else:
            pl.when(condition)(copy.wait_send)
    for k in range(chips):
        for index in range(2 * pieces):
            pl.when(not_last)(down_copy(k, index).wait_send)
            pl.when(not_first)(up_copy(k, index).wait_send)
            result_copy(k, index).wait()
    for store in stores:
        store.wait()


def rotate(inputs, out_grads, act_basis, grad_basis):
    rows, cols = lax.axis_size("row"), lax.axis_size("col")
    chips = cols // 2
    tok = inputs.shape[0]
    total_tok = rows * cols * tok
    act_depth, act_width = act_basis.shape
    grad_depth, grad_width = grad_basis.shape
    bf16 = jnp.bfloat16
    vmem, dma = pltpu.VMEM, pltpu.SemaphoreType.DMA
    rot_grads, rot_inputs = pl.pallas_call(
        functools.partial(rotate_kernel, rows, cols),
        out_shape=(
            jax.ShapeDtypeStruct((rows, chips, 2, tok, grad_width), bf16),
            jax.ShapeDtypeStruct((rows, chips, 2, tok, act_width), bf16),
        ),
        in_specs=[
            pl.BlockSpec(memory_space=pltpu.VMEM),
            pl.BlockSpec(memory_space=pltpu.VMEM),
            pl.BlockSpec(memory_space=pl.ANY),
            pl.BlockSpec(memory_space=pl.ANY),
        ],
        out_specs=(pl.BlockSpec(memory_space=pl.ANY), pl.BlockSpec(memory_space=pl.ANY)),
        scratch_shapes=[
            vmem((rows, chips, 2, tok, grad_depth), bf16),
            vmem((chips, 2, rows, tok, act_depth), bf16),
            vmem(act_basis.shape, bf16),
            vmem(grad_basis.shape, bf16),
            vmem((rows, chips, 2, tok, grad_width), bf16),
            vmem((rows, chips, tok, grad_width), bf16),
            vmem((rows, chips, tok, grad_width), bf16),
            vmem((rows, chips, 2, tok, grad_width), bf16),
            vmem((chips, 2, rows, tok, act_width), bf16),
            vmem((chips, 2, rows, tok, act_width), bf16),
            vmem((chips, 2, rows, tok, act_width), bf16),
            dma((2,)), dma((rows + 2 * cols,)),
            dma((rows,)), dma((rows,)), dma((cols,)), dma((cols,)),
            dma((chips,)), dma((chips,)), dma((chips,)), dma((chips,)),
            dma((rows,)), dma((rows,)), dma((rows,)),
            dma((rows,)), dma((rows,)),
            dma((rows, chips)), dma((rows, chips)), dma((rows, chips)), dma((rows, chips)),
            dma((rows,)), dma((rows,)),
            dma((chips, 4)), dma((chips, 4)), dma((chips, 4)), dma((chips, 4)),
        ],
        compiler_params=pltpu.CompilerParams(
            collective_id=0, has_side_effects=True, vmem_limit_bytes=58 * MIB
        ),
        cost_estimate=pl.CostEstimate(
            flops=2 * total_tok * (act_depth * act_width + grad_depth * grad_width),
            bytes_accessed=4 * (act_depth * act_width + grad_depth * grad_width),
            transcendentals=0,
        ),
    )(inputs, out_grads, act_basis, grad_basis)
    return rot_grads.reshape(total_tok, grad_width), rot_inputs.reshape(total_tok, act_width)


def shards(seq_ids, attn_weights, values, out_grads, act_basis, grad_basis):
    total_tok = seq_ids.shape[0]
    sequences = total_tok // SEQ_MEAN
    inputs = attention(seq_ids, attn_weights, values)
    rot_grads, rot_inputs = rotate(inputs, out_grads, act_basis, grad_basis)
    seq_range = jnp.arange(sequences + 1, dtype=jnp.int32)
    bounds = jnp.sum((seq_ids[None, :] < seq_range[:, None]).astype(jnp.int32), axis=1)
    return fit(bounds, rot_grads, rot_inputs, sequences)

def solution(mesh):
    return jax.shard_map(
        shards,
        mesh=mesh,
        in_specs=(
            P(),
            P(("row", "col"), None, None),
            P(("row", "col"), None),
            P(("row", "col"), None),
            P("row", "col"),
            P("col", "row"),
        ),
        out_specs=P("row", "col"),
        check_vma=False,
    )
```

```python
import functools
import jax
import jax.numpy as jnp
from jax import lax
from jax.experimental import pallas as pl
from jax.experimental.pallas import tpu as pltpu
from jax.sharding import PartitionSpec as P

SEQ_MEAN = 128
LONGEST = 192
MIB = 1 << 20


def from_behind(value, axis, steps):
    count = lax.axis_size(axis)
    initial, last = (max(0, -steps), min(count, count - steps))
    return lax.ppermute(value, axis, [(source, source + steps) for source in range(initial, last)])


def fit_kernel(sequences, window, bounds_ref, grads_ref, acts_ref, out_ref):
    total_tok = grads_ref.shape[0]
    positions = lax.broadcasted_iota(jnp.int32, (window, 1), 0)

    def tile(index):
        start, end = bounds_ref[index], bounds_ref[index + 1]
        first = pl.multiple_of(jnp.minimum(start // 16 * 16, total_tok - window), 16)
        here = positions + first
        inside = jnp.logical_and(here >= start, here < end)
        grads = grads_ref[pl.ds(first, window), :]
        grads = jnp.where(inside, grads, jnp.zeros_like(grads))
        acts = acts_ref[pl.ds(first, window), :]
        product = lax.dot_general(
            grads, acts, (((0,), (0,)), ((), ())), preferred_element_type=jnp.float32
        )
        return product * product

    group = 4

    def squares(index):
        total = tile(index)
        for step in range(1, group):
            total = total + tile(index + step)
        return total

    out_ref[...] = squares(0)

    @pl.loop(1, sequences // group - 1)
    def _(index):
        out_ref[...] += squares(index * group)

    out_ref[...] = (out_ref[...] + squares(sequences - group)) * (1.0 / sequences)


def fit(bounds, rot_grads, rot_inputs, sequences):
    total_tok, rows = rot_grads.shape
    columns = rot_inputs.shape[1]
    height = 256
    window = (LONGEST + 15 + 127) // 128 * 128
    return pl.pallas_call(
        functools.partial(fit_kernel, sequences, window),
        grid=(rows // height,),
        out_shape=jax.ShapeDtypeStruct((rows, columns), jnp.float32),
        in_specs=[
            pl.BlockSpec(memory_space=pltpu.SMEM),
            pl.BlockSpec((total_tok, height), lambda i: (0, i)),
            pl.BlockSpec((total_tok, columns), lambda i: (0, 0)),
        ],
        out_specs=pl.BlockSpec((height, columns), lambda i: (i, 0)),
        compiler_params=pltpu.CompilerParams(vmem_limit_bytes=58 * MIB),
        cost_estimate=pl.CostEstimate(
            flops=2 * rows * columns * window * sequences,
            bytes_accessed=4 * rows * columns + 2 * total_tok * (rows + columns),
            transcendentals=0,
        ),
    )(bounds, rot_grads, rot_inputs)


def attention(seq_ids, attn_weights, values):
    tok = values.shape[0]
    width = values.shape[1]
    heads = attn_weights.shape[1]
    window = attn_weights.shape[2]
    head_size = width // heads
    offset = lax.axis_index(("row", "col")) * tok
    previous = from_behind(values, ("row", "col"), 1)
    keys = jnp.concatenate([previous, values], axis=0).reshape(2 * tok, heads, head_size)
    query_pos = offset + jnp.arange(tok, dtype=jnp.int32)
    steps_back = jnp.arange(window, dtype=jnp.int32)
    query_seg = lax.dynamic_slice_in_dim(seq_ids, offset, tok, 0)
    run_start = jnp.sum((seq_ids[None, :] < query_seg[:, None]).astype(jnp.int32), axis=1)
    valid = (steps_back[None, :] <= (query_pos - run_start)[:, None]).astype(jnp.float32)
    masked = attn_weights * valid[:, None, :]
    probs = (masked / jnp.sum(masked, axis=2, keepdims=True)).astype(jnp.bfloat16)
    local_key = tok + jnp.arange(tok, dtype=jnp.int32)[:, None] - steps_back[None, :]
    selector = (
        local_key[:, :, None] == jnp.arange(2 * tok, dtype=jnp.int32)[None, None, :]
    ).astype(jnp.bfloat16)
    spread = jnp.einsum("phj,pjk->phk", probs, selector, preferred_element_type=jnp.float32).astype(
        jnp.bfloat16
    )
    mixed = jnp.einsum("phk,khd->phd", spread, keys, preferred_element_type=jnp.float32)
    return mixed.reshape(tok, width).astype(jnp.bfloat16)


MESH = pl.DeviceIdType.MESH


def merged(first, second):
    steps = [((i + 0.5) / len(first), 0, s) for i, s in enumerate(first)]
    steps += [((i + 0.5) / len(second), 1, s) for i, s in enumerate(second)]
    return [s for _, _, s in sorted(steps, key=lambda entry: entry[:2])]


def rotate_kernel(
    rows, cols, inputs_ref, grads_ref, act_hbm, grad_hbm, rot_grads_ref, rot_inputs_ref,
    grad_all, act_all, act_basis, grad_basis, part, pair, ring, rot_grads, act_part, down, up,
    local_sem, out_sem, a1_send, a1_recv, g1_send, g1_recv, a2_send, a2_recv, af_send, af_recv,
    g2_down, g2_up, g2_recv, pair_send, pair_recv, ring_send, ring_recv, ag_send, ag_recv,
    agf_send, agf_recv, down_send, down_recv, up_send, up_recv,
):
    chips = cols // 2
    tok = inputs_ref.shape[0]
    act_depth, act_width = act_basis.shape
    grad_depth, grad_width = grad_basis.shape
    r, c = lax.axis_index("row"), lax.axis_index("col")
    chip, core = c // 2, c % 2
    partner = (r, 2 * chip + 1 - core)
    not_last, not_first = r < rows - 1, r > 0
    pending = []

    def remote(src, dst, send, recv, device):
        return pltpu.make_async_remote_copy(
            src_ref=src, dst_ref=dst, send_sem=send, recv_sem=recv, device_id=device,
            device_id_type=MESH,
        )

    def send(copy, condition=None):
        pending.append((copy, condition))
        if condition is None:
            copy.start()
        else:
            pl.when(condition)(copy.start)

    def arrived(dst, recv, condition=None):
        copy = remote(dst, dst, recv, recv, partner)
        if condition is None:
            copy.wait_recv()
        else:
            pl.when(condition)(copy.wait_recv)

    load_grad = pltpu.make_async_copy(grad_hbm, grad_basis, local_sem.at[0])
    load_act = pltpu.make_async_copy(act_hbm, act_basis, local_sem.at[1])
    load_grad.start()
    load_act.start()

    other_rows = [(r + d) % rows for d in range(1, rows)]
    other_cols = [(c + d) % cols for d in range(1, cols)]
    other_chips = [(chip + d) % chips for d in range(1, chips)]
    barrier = pltpu.get_barrier_semaphore()
    for other in other_rows:
        pl.semaphore_signal(barrier, inc=1, device_id=(other, c), device_id_type=MESH)
    for other in other_cols:
        pl.semaphore_signal(barrier, inc=1, device_id=(r, other), device_id_type=MESH)
    pl.semaphore_wait(barrier, rows + cols - 2)

    def act_columns(row):
        return inputs_ref.at[:, pl.ds(pl.multiple_of(row * act_depth, act_depth), act_depth)]

    def grad_columns(col):
        return grads_ref.at[:, pl.ds(pl.multiple_of(col * grad_depth, grad_depth), grad_depth)]

    for other in other_rows:
        send(remote(act_columns(other), act_all.at[chip, core, r], a1_send.at[other],
                    a1_recv.at[r], (other, c)))
    for other in other_cols:
        send(remote(grad_columns(other), grad_all.at[r, chip, core], g1_send.at[other],
                    g1_recv.at[c], (r, other)))
    act_all[chip, core, r] = act_columns(r)[...]
    grad_all[r, chip, core] = grad_columns(c)[...]

    for other in other_rows:
        arrived(act_all.at[chip, core, other], a1_recv.at[other])
    for other in other_chips:
        send(remote(act_all.at[chip, core], act_all.at[chip, core], a2_send.at[other],
                    a2_recv.at[chip], (r, 2 * other + core)))
    send(remote(act_all.at[chip, core], act_all.at[chip, core], af_send.at[chip],
                af_recv.at[chip], partner))
    for other in other_cols:
        arrived(grad_all.at[r, other // 2, other % 2], g1_recv.at[other])

    order = [sorted(range(rows), key=lambda b: (abs(b - row), b)) for row in range(rows)]
    blocks = []
    for slot in range(rows):
        block = 0
        for row in range(rows):
            block = block + jnp.where(r == row, order[row][slot], 0)
        blocks.append(block)

    def grad_rotate(slot):
        block = blocks[slot]
        if slot > 0:
            arrived(grad_all.at[block], g2_recv.at[block])
        send(remote(grad_all.at[block], grad_all.at[block], g2_down.at[slot], g2_recv.at[block],
                    (jnp.minimum(r + 1, rows - 1), c)),
             jnp.logical_and(block <= r, not_last))
        send(remote(grad_all.at[block], grad_all.at[block], g2_up.at[slot], g2_recv.at[block],
                    (jnp.maximum(r - 1, 0), c)),
             jnp.logical_and(block >= r, not_first))
        if slot == 0:
            load_grad.wait()
        width = min(512, grad_width)

        @pl.loop(0, grad_width // width)
        def _(j):
            at = pl.ds(pl.multiple_of(j * width, width), width)
            term = jnp.dot(
                grad_all[block].reshape(cols * tok, grad_depth), grad_basis[:, at],
                preferred_element_type=jnp.float32,
            )
            part[block, :, :, :, at] = term.astype(jnp.bfloat16).reshape(chips, 2, tok, width)

        send(remote(part.at[block, :, 1 - core], pair.at[block], pair_send.at[slot],
                    pair_recv.at[block], partner))

    def grad_pair(slot):
        block = blocks[slot]
        arrived(pair.at[block], pair_recv.at[block])

        @pl.loop(0, chips)
        def _(k):
            total = part[block, k, core].astype(jnp.float32) + pair[block, k].astype(jnp.float32)
            part[block, k, core] = total.astype(jnp.bfloat16)

        for other in other_chips:
            send(remote(part.at[block, other, core], ring.at[block, chip],
                        ring_send.at[slot, other], ring_recv.at[block, chip],
                        (r, 2 * other + core)))

    def grad_sum(slot):
        block = blocks[slot]
        for other in other_chips:
            arrived(ring.at[block, other], ring_recv.at[block, other])
        width = min(512, grad_width)

        @pl.loop(0, grad_width // width)
        def _(j):
            at = pl.ds(pl.multiple_of(j * width, width), width)
            total = part[block, chip, core, :, at].astype(jnp.float32)
            for other in other_chips:
                total = total + ring[block, other, :, at].astype(jnp.float32)
            rot_grads[block, chip, core, :, at] = total.astype(jnp.bfloat16)

        for other in other_chips:
            send(remote(rot_grads.at[block, chip, core], rot_grads.at[block, chip, core],
                        ag_send.at[slot, other], ag_recv.at[block, chip],
                        (r, 2 * other + core)))

    def grad_share(slot):
        block = blocks[slot]
        for other in other_chips:
            arrived(rot_grads.at[block, other, core], ag_recv.at[block, other])
        send(remote(rot_grads.at[block, :, core], rot_grads.at[block, :, core],
                    agf_send.at[slot], agf_recv.at[block], partner))

    def grad_tick(tick):
        if tick < rows:
            grad_rotate(tick)
        if 0 <= tick - 1 < rows:
            grad_pair(tick - 1)
        if 0 <= tick - 2 < rows:
            grad_sum(tick - 2)
        if 0 <= tick - 3 < rows:
            grad_share(tick - 3)

    def act_rotate(step):
        k = (chip + step) % chips
        if step > 0:
            arrived(act_all.at[k, core], a2_recv.at[k])
            send(remote(act_all.at[k, core], act_all.at[k, core], af_send.at[k], af_recv.at[k],
                        partner))
        arrived(act_all.at[k, 1 - core], af_recv.at[k])
        if step == 0:
            load_act.wait()
        width = min(512, act_width)

        @pl.loop(0, act_width // width)
        def _(j):
            at = pl.ds(pl.multiple_of(j * width, width), width)
            term = jnp.dot(
                act_all[k].reshape(2 * rows * tok, act_depth), act_basis[:, at],
                preferred_element_type=jnp.float32,
            )
            act_part[k, :, :, :, at] = term.astype(jnp.bfloat16).reshape(2, rows, tok, width)

        @pl.when(r == 0)
        def _():
            down[k] = act_part[k]

        @pl.when(r == rows - 1)
        def _():
            up[k] = act_part[k]

        for half in range(2):
            pl.when(r == 0)(down_copy(k, half).start)
            pl.when(r == rows - 1)(up_copy(k, half).start)

    def down_copy(k, half):
        return remote(down.at[k, half], down.at[k, half], down_send.at[k, half],
                      down_recv.at[k, half], (jnp.minimum(r + 1, rows - 1), c))

    def up_copy(k, half):
        return remote(up.at[k, half], up.at[k, half], up_send.at[k, half],
                      up_recv.at[k, half], (jnp.maximum(r - 1, 0), c))

    def result_copy(k, half):
        return pltpu.make_async_copy(
            act_part.at[k, half], rot_inputs_ref.at[:, k, half], out_sem.at[rows + 2 * k + half]
        )

    def chain_step(flow, other, copy, index, has_next, is_second):
        k, half = (chip + index // 2) % chips, index % 2
        copy(k, half).wait_recv()

        @pl.when(is_second)
        def _():
            @pl.loop(0, rows)
            def _(q):
                before = flow[k, half, q].astype(jnp.float32)
                own = act_part[k, half, q].astype(jnp.float32)
                rest = other[k, half, q].astype(jnp.float32)
                flow[k, half, q] = (before + own).astype(jnp.bfloat16)
                act_part[k, half, q] = (before + rest).astype(jnp.bfloat16)

        @pl.when(jnp.logical_not(is_second))
        def _():
            @pl.loop(0, rows)
            def _(q):
                before = flow[k, half, q].astype(jnp.float32)
                own = act_part[k, half, q].astype(jnp.float32)
                flow[k, half, q] = (before + own).astype(jnp.bfloat16)

        pl.when(has_next)(copy(k, half).start)
        pl.when(is_second)(result_copy(k, half).start)

    upper = 2 * r >= rows

    def act_chain(time):
        below, above = time - r, time - (rows - 1 - r)

        @pl.when(jnp.logical_and(not_first, jnp.logical_and(below >= 0, below < cols)))
        def _():
            chain_step(down, up, down_copy, below, not_last, upper)

        @pl.when(jnp.logical_and(not_last, jnp.logical_and(above >= 0, above < cols)))
        def _():
            chain_step(up, down, up_copy, above, not_first, jnp.logical_not(upper))

    stores = []
    ticks = [functools.partial(grad_tick, t) for t in range(rows + 3)]
    rotates = [functools.partial(act_rotate, s) for s in range(chips)]
    chains = [functools.partial(act_chain, t) for t in range(1, cols + rows - 1)]
    early = rows // 2
    for step in merged(ticks[:early], rotates[:-1]) + rotates[-1:] + merged(chains, ticks[early:]):
        step()
    for slot in range(rows):
        block = blocks[slot]
        arrived(rot_grads.at[block, :, 1 - core], agf_recv.at[block])
        store = pltpu.make_async_copy(rot_grads.at[block], rot_grads_ref.at[block], out_sem.at[slot])
        store.start()
        stores.append(store)
    for copy, condition in pending:
        if condition is None:
            copy.wait_send()
        else:
            pl.when(condition)(copy.wait_send)
    for k in range(chips):
        for half in range(2):
            pl.when(not_last)(down_copy(k, half).wait_send)
            pl.when(not_first)(up_copy(k, half).wait_send)
            result_copy(k, half).wait()
    for store in stores:
        store.wait()


def rotate(inputs, out_grads, act_basis, grad_basis):
    rows, cols = lax.axis_size("row"), lax.axis_size("col")
    chips = cols // 2
    tok = inputs.shape[0]
    total_tok = rows * cols * tok
    act_depth, act_width = act_basis.shape
    grad_depth, grad_width = grad_basis.shape
    bf16 = jnp.bfloat16
    vmem, dma = pltpu.VMEM, pltpu.SemaphoreType.DMA
    rot_grads, rot_inputs = pl.pallas_call(
        functools.partial(rotate_kernel, rows, cols),
        out_shape=(
            jax.ShapeDtypeStruct((rows, chips, 2, tok, grad_width), bf16),
            jax.ShapeDtypeStruct((rows, chips, 2, tok, act_width), bf16),
        ),
        in_specs=[
            pl.BlockSpec(memory_space=pltpu.VMEM),
            pl.BlockSpec(memory_space=pltpu.VMEM),
            pl.BlockSpec(memory_space=pl.ANY),
            pl.BlockSpec(memory_space=pl.ANY),
        ],
        out_specs=(pl.BlockSpec(memory_space=pl.ANY), pl.BlockSpec(memory_space=pl.ANY)),
        scratch_shapes=[
            vmem((rows, chips, 2, tok, grad_depth), bf16),
            vmem((chips, 2, rows, tok, act_depth), bf16),
            vmem(act_basis.shape, bf16),
            vmem(grad_basis.shape, bf16),
            vmem((rows, chips, 2, tok, grad_width), bf16),
            vmem((rows, chips, tok, grad_width), bf16),
            vmem((rows, chips, tok, grad_width), bf16),
            vmem((rows, chips, 2, tok, grad_width), bf16),
            vmem((chips, 2, rows, tok, act_width), bf16),
            vmem((chips, 2, rows, tok, act_width), bf16),
            vmem((chips, 2, rows, tok, act_width), bf16),
            dma((2,)), dma((rows + cols,)),
            dma((rows,)), dma((rows,)), dma((cols,)), dma((cols,)),
            dma((chips,)), dma((chips,)), dma((chips,)), dma((chips,)),
            dma((rows,)), dma((rows,)), dma((rows,)),
            dma((rows,)), dma((rows,)),
            dma((rows, chips)), dma((rows, chips)), dma((rows, chips)), dma((rows, chips)),
            dma((rows,)), dma((rows,)),
            dma((chips, 2)), dma((chips, 2)), dma((chips, 2)), dma((chips, 2)),
        ],
        compiler_params=pltpu.CompilerParams(
            collective_id=0, has_side_effects=True, vmem_limit_bytes=58 * MIB
        ),
        cost_estimate=pl.CostEstimate(
            flops=2 * total_tok * (act_depth * act_width + grad_depth * grad_width),
            bytes_accessed=4 * (act_depth * act_width + grad_depth * grad_width),
            transcendentals=0,
        ),
    )(inputs, out_grads, act_basis, grad_basis)
    return rot_grads.reshape(total_tok, grad_width), rot_inputs.reshape(total_tok, act_width)


def shards(seq_ids, attn_weights, values, out_grads, act_basis, grad_basis):
    total_tok = seq_ids.shape[0]
    sequences = total_tok // SEQ_MEAN
    inputs = attention(seq_ids, attn_weights, values)
    rot_grads, rot_inputs = rotate(inputs, out_grads, act_basis, grad_basis)
    seq_range = jnp.arange(sequences + 1, dtype=jnp.int32)
    bounds = jnp.sum((seq_ids[None, :] < seq_range[:, None]).astype(jnp.int32), axis=1)
    return fit(bounds, rot_grads, rot_inputs, sequences)

def solution(mesh):
    return jax.shard_map(
        shards,
        mesh=mesh,
        in_specs=(
            P(),
            P(("row", "col"), None, None),
            P(("row", "col"), None),
            P(("row", "col"), None),
            P("row", "col"),
            P("col", "row"),
        ),
        out_specs=P("row", "col"),
        check_vma=False,
    )
```
